256 devices in a mesh: row: 16 (over z, y_lo), col: 16 (over y_hi, x, core).
Axes of the slice: x: 4, y: 4 (y_hi: 2, y_lo: 2; y = y_hi * 2 + y_lo), z: 8, core: 2. Of those that a mesh axis runs over, the one named last changes fastest.
Arguments:
- separator_inverse: float32 [6144, 6144], P('row', 'col')
- panels: float32 [6144, 2048], P(('row', 'col')), as said below
- diag_inverse: float32 [2, 1024, 1024], P(None, ('row', 'col'))
- ancestors: int32 [2, 6], replicated, may hold values from 0 to 47, as said below
Outputs:
- off_blocks: float32 [6144, 2048], P(('row', 'col'))
- diag_blocks: float32 [2, 1024, 1024], P(None, ('row', 'col'))
The draws below stay inside these ranges and needn't reach their ends.
Inputs may be any that keep to these rules, and one draw needn't show every extreme that they name: `ancestors`: each row holds 6 different tile rows of the separator in rising order. `panels`: rows of supernode s's columns are zero outside the tiles listed in ancestors[s].
All inputs are finite; a program needn't handle non-finite values.
Results may differ from the reference program's by a relative error of at most 0.00007.
Values sent between devices are 32-bit elements; how exact they have to be, the bound alone decides.
A program may use at most 64 MiB of HBM per device.

```python
import jax
import jax.numpy as jnp
from jax import lax

W = 1024
B = 128
NST = 48
NS = 6144
NA = 6


def ancestor_lists(key):
    rows_out = []
    for member in range(2):
        subkey = jax.random.fold_in(key, 11 + member)
        scores = jax.random.permutation(subkey, NST).astype(jnp.int32)
        tile_ids = jnp.arange(NST, dtype=jnp.int32)
        run_len = max(1, NA // 2)
        stride = max(1, NST // run_len)
        forced = tile_ids % stride == stride - 1
        scores = jnp.where(forced, tile_ids - 2 * NST, scores)
        order = jnp.argsort(scores, stable=True).astype(jnp.int32)
        rows_out.append(jnp.sort(order[:NA]))
    return jnp.stack(rows_out).astype(jnp.int32)


def draw_ancestors(key, part):
    return ancestor_lists(key)


def draw_panels(key, part):
    lists = ancestor_lists(key)
    key = jax.random.fold_in(key, 21)
    values = jax.random.normal(key, (NS, 2, W), jnp.float32)
    tile_ids = jnp.arange(NS, dtype=jnp.int32) // B
    is_live = jnp.any(tile_ids[:, None, None] == lists[None, :, :], axis=2).astype(jnp.float32)
    values = values * is_live[:, :, None] / jnp.sqrt(jnp.float32(NA * B))
    return values.reshape(NS, 2 * W)


def draw_separator_inverse(key, part):
    key = jax.random.fold_in(key, 31)
    first, second = jax.random.split(key)
    raw = jax.random.normal(first, (NS, NS), jnp.float32)
    middle = jax.random.uniform(second, (NS,), jnp.float32, 3.0, 4.0)
    general = raw * 0.5
    index = jnp.arange(NS, dtype=jnp.int32)
    return jnp.where(index[:, None] == index[None, :], middle[:, None], general)


def draw_diag_inverse(key, part):
    key = jax.random.fold_in(key, 41)
    first, second = jax.random.split(key)
    raw = jax.random.normal(first, (2, W, W), jnp.float32)
    middle = jax.random.uniform(second, (2, W), jnp.float32, 1.0, 2.0)
    sym = (raw + jnp.swapaxes(raw, 1, 2)) * 0.2
    index = jnp.arange(W, dtype=jnp.int32)
    same = index[:, None] == index[None, :]
    return jnp.where(same[None, :, :], middle[:, :, None], sym)


def setup_inputs(seed: int = 0) -> dict:
    streams_of = jax.random.split(jax.random.key(seed), 5)
    return {
        "separator_inverse": draw_separator_inverse(jax.random.fold_in(streams_of[4], 71), 0),
        "panels": draw_panels(jax.random.fold_in(streams_of[4], 71), 0),
        "diag_inverse": draw_diag_inverse(jax.random.fold_in(streams_of[4], 71), 0),
        "ancestors": draw_ancestors(jax.random.fold_in(streams_of[4], 71), 0),
    }


HIGHEST = lax.Precision.HIGHEST


def reference(separator_inverse, panels, diag_inverse, ancestors):
    products = jnp.dot(separator_inverse, panels, precision=HIGHEST, preferred_element_type=jnp.float32)
    tile_ids = (jnp.arange(NS, dtype=jnp.int32) // B).astype(jnp.int32)
    is_live = jnp.any(tile_ids[:, None, None] == ancestors[None, :, :], axis=2).astype(jnp.float32)
    shaped = products.reshape(NS, 2, W)
    off_blocks = -(shaped * is_live[:, :, None]).reshape(NS, 2 * W)
    quadratic = jnp.einsum("nsi,nsj->sij", panels.reshape(NS, 2, W), shaped, precision=HIGHEST)
    return off_blocks, diag_inverse + quadratic
```

```python
import jax
import jax.numpy as jnp
from jax import lax
from jax.experimental import pallas as pl
from jax.experimental.pallas import tpu as pltpu
from jax.sharding import PartitionSpec as P

MESH = pl.DeviceIdType.MESH
F32 = jnp.float32
BF16 = jnp.bfloat16
N = 16
HALF = 8
NT = 48
NA = 6
T = 128

S1, P1, X2, Y2, S2, S3, Q4, O4, D5 = range(9)


def split(x):
    high = x.astype(BF16)
    return high, (x - high.astype(F32)).astype(BF16)


def dot3(a, b):
    ah, al = a
    bh, bl = b
    dot = lambda u, v: jnp.dot(u, v, preferred_element_type=F32)
    return dot(ah, bh) + (dot(ah, bl) + dot(al, bh))


def kernel(
    anc,
    sep,
    pan,
    off,
    quad,
    s_rows,
    p_rows,
    p_unit,
    x_buf,
    y_buf,
    s_by_tile,
    s_col,
    s_tiles,
    s_unit,
    s_fin,
    q_unit,
    q_buf,
    off_st,
    d_st,
    y_hi,
    y_lo,
    send,
    recv,
):
    r = lax.axis_index("row")
    c = lax.axis_index("col")
    s = lax.div(r, HALF)
    b = lax.rem(r, HALF)

    def remote(src, dst, i, device):
        return pltpu.make_async_remote_copy(
            src_ref=src,
            dst_ref=dst,
            send_sem=send.at[i],
            recv_sem=recv.at[i],
            device_id=device,
            device_id_type=MESH,
        )

    def push(src, dst, i, dr, dc):
        here = jnp.logical_and(dr == r, dc == c)

        @pl.when(here)
        def _():
            pltpu.make_async_copy(src, dst, recv.at[i]).start()

        @pl.when(jnp.logical_not(here))
        def _():
            remote(src, dst, i, (dr, dc)).start()

    def take(sem, ref):
        pltpu.make_async_copy(ref, ref, sem).wait()

    def loop(lo, hi, body):
        def step(i, carry):
            body(i)
            return carry

        lax.fori_loop(lo, hi, step, 0)

    def send_s(i):
        d = lax.rem(c + i, N)
        remote(sep.at[:, pl.ds(8 * d, 8), :], s_rows.at[c], S1, (r, d)).start()

    loop(1, N, send_s)
    pltpu.make_async_copy(sep.at[:, pl.ds(8 * c, 8), :], s_rows.at[c], recv.at[S1]).start()

    for q in range(3):
        piece = 3 * c + q
        m = lax.div(piece, N)
        o = lax.rem(piece, N)

        def send_p(i, q=q, m=m, o=o):
            d = lax.rem(r + i, N)
            push(pan.at[q, :, pl.ds(pl.multiple_of(T * d, T), T)], p_rows.at[3 * r + m], P1, d, o)

        loop(0, N, send_p)

    take(recv.at[P1], p_rows)
    for k in range(NA):
        p_unit[k] = p_rows[anc[s, k]]

    def send_x(i):
        d = lax.rem(c + i, N)
        remote(p_unit, x_buf.at[:, c], X2, (r, d)).start()

    loop(1, N, send_x)
    x_buf[:, pl.ds(c, 1)] = p_unit[...][:, None]

    def send_y(i):
        dr = HALF * s + lax.rem(b + lax.div(i, 2), HALF)
        push(p_unit, y_buf.at[:, c], Y2, dr, 2 * b + lax.rem(i, 2))

    loop(0, 2 * HALF, send_y)

    take(recv.at[S1], s_rows)
    for j in range(N):
        for v in range(3):
            s_by_tile[3 * j + v] = s_rows[j, :, :, T * v : T * v + T]
    for t in range(2):
        for l in range(NA):
            s_col[t, l] = s_by_tile[anc[t, l]]

    def send_s2(i):
        t = lax.div(i, NA)
        l = lax.rem(i, NA)
        push(s_col.at[t, l], s_tiles.at[pl.ds(3 * r, 3)], S2, HALF * t + l, c)

    loop(0, 2 * NA, send_s2)

    @pl.when(b < NA)
    def _():
        take(recv.at[S2], s_tiles)
        for k in range(NA):
            s_unit[k] = s_tiles[anc[s, k]]

        def send_s3(i):
            d = HALF * s + lax.rem(b + i, HALF)
            remote(s_unit, s_fin.at[b], S3, (d, c)).start()

        loop(1, HALF, send_s3)
        pltpu.make_async_copy(s_unit, s_fin.at[b], recv.at[S3]).start()

    take(recv.at[Y2], y_buf)
    for k in range(NA):
        yt = y_buf[k].reshape(T, T).T
        hi, lo = split(yt)
        y_hi[k] = hi
        y_lo[k] = lo

    take(recv.at[X2], x_buf.at[:, pl.ds(0, N - 1)])
    take(recv.at[S3], s_fin)
    acc = jnp.zeros((NA * 8, T), F32)
    for l in range(NA):
        acc += dot3(split(s_fin[l].reshape(NA * 8, T)), split(x_buf[l].reshape(T, T)))
    q_unit[pl.ds(0, NA)] = acc.reshape(NA, 8, T)
    q_unit[NA] = jnp.zeros((8, T), F32)

    def send_q(i):
        d = lax.rem(c + i, N)
        remote(q_unit.at[pl.ds(0, NA)], q_buf.at[:, c], Q4, (r, d)).start()

    loop(1, N, send_q)
    q_buf[:, pl.ds(c, 1)] = q_unit[pl.ds(0, NA)][:, None]

    for t in range(NT):
        place = NA
        for k in range(NA):
            place = jnp.minimum(place, NA - (anc[s, k] == t).astype(jnp.int32) * (NA - k))
        off_st[t] = -q_unit[place]

    def send_off(i):
        t = lax.rem(3 * r + i, NT)
        piece = N * lax.rem(t, 3) + c
        dst = off.at[lax.rem(piece, 3), :, pl.ds(pl.multiple_of(T * r, T), T)]
        push(off_st.at[t], dst, O4, lax.div(t, 3), lax.div(piece, 3))

    loop(0, NT, send_off)

    take(recv.at[Q4], q_buf.at[:, pl.ds(0, N - 1)])
    rows = pl.ds(pl.multiple_of(lax.rem(c, 2) * 64, 64), 64)
    acc = jnp.zeros((64, T), F32)
    for k in range(NA):
        acc += dot3((y_hi[k, rows, :], y_lo[k, rows, :]), split(q_buf[k].reshape(T, T)))
    d_st[...] = acc.reshape(N, 4, T)

    def send_d(i):
        d = lax.rem(c + i, N)
        push(d_st.at[d], quad.at[r], D5, c, d)

    loop(0, N, send_d)

    take(send.at[S1], s_rows.at[pl.ds(0, N - 1)])
    take(send.at[X2], x_buf.at[:, pl.ds(0, N - 1)])
    take(send.at[Q4], q_buf.at[:, pl.ds(0, N - 1)])

    @pl.when(b < NA)
    def _():
        take(send.at[S3], s_tiles.at[pl.ds(0, 7 * NA)])
        take(send.at[S2], s_tiles.at[pl.ds(0, 33)])

    @pl.when(b >= NA)
    def _():
        take(send.at[S2], s_tiles.at[pl.ds(0, 36)])

    own = jnp.logical_or(jnp.logical_or(c == 0, c == 7), jnp.logical_or(c == 8, c == 15))

    @pl.when(own)
    def _():
        take(send.at[P1], p_rows.at[pl.ds(0, NT - 1)])
        take(send.at[O4], p_rows.at[pl.ds(0, NT - 1)])

    @pl.when(jnp.logical_not(own))
    def _():
        take(send.at[P1], p_rows)
        take(send.at[O4], p_rows)

    @pl.when(lax.div(c, 2) == b)
    def _():
        take(send.at[Y2], y_buf.at[:, pl.ds(0, N - 1)])

    @pl.when(lax.div(c, 2) != b)
    def _():
        take(send.at[Y2], y_buf)

    @pl.when(r == c)
    def _():
        take(send.at[D5], d_st.at[pl.ds(0, N - 1)])

    @pl.when(r != c)
    def _():
        take(send.at[D5], d_st)

    take(recv.at[O4], off)
    take(recv.at[D5], quad)


def per_device(separator_inverse, panels, diag_inverse, ancestors):
    hbm = pl.BlockSpec(memory_space=pl.ANY)
    vmem = pltpu.VMEM
    off, quad = pl.pallas_call(
        kernel,
        out_shape=(
            jax.ShapeDtypeStruct((3, 8, 2 * HALF * T), F32),
            jax.ShapeDtypeStruct((N, 4, T), F32),
        ),
        in_specs=[pl.BlockSpec(memory_space=pltpu.SMEM), hbm, hbm],
        out_specs=(hbm, pl.BlockSpec(memory_space=pltpu.VMEM)),
        scratch_shapes=[
            vmem((N, 3, 8, 3 * T), F32),
            vmem((NT, 8, T), F32),
            vmem((NA, 8, T), F32),
            vmem((NA, N, 8, T), F32),
            vmem((NA, N, 8, T), F32),
            vmem((NT, 3, 8, T), F32),
            vmem((2, NA, 3, 8, T), F32),
            vmem((NT, 8, T), F32),
            vmem((NA, 8, T), F32),
            vmem((NA, NA, 8, T), F32),
            vmem((NA + 1, 8, T), F32),
            vmem((NA, N, 8, T), F32),
            vmem((NT, 8, T), F32),
            vmem((N, 4, T), F32),
            vmem((NA, T, T), BF16),
            vmem((NA, T, T), BF16),
            pltpu.SemaphoreType.DMA((9,)),
            pltpu.SemaphoreType.DMA((9,)),
        ],
        compiler_params=pltpu.CompilerParams(has_side_effects=True),
        name="selected_inverse",
    )(
        ancestors,
        separator_inverse.reshape(3, T, 3 * T),
        panels.reshape(3, 8, 2 * HALF * T),
    )
    quad_rows = quad.reshape(2, HALF, 4, T).transpose(0, 2, 1, 3).reshape(2, 4, HALF * T)
    return off.reshape(24, 2 * HALF * T), diag_inverse + quad_rows


def solution(mesh):
    return jax.shard_map(
        per_device,
        mesh=mesh,
        in_specs=(P("row", "col"), P(("row", "col"), None), P(None, ("row", "col"), None), P()),
        out_specs=(P(("row", "col"), None), P(None, ("row", "col"), None)),
        check_vma=False,
    )
```

```python
import jax
import jax.numpy as jnp
from jax import lax
from jax.experimental import pallas as pl
from jax.experimental.pallas import tpu as pltpu
from jax.sharding import PartitionSpec as P

MESH = pl.DeviceIdType.MESH
F32 = jnp.float32
BF16 = jnp.bfloat16
N = 16
HALF = 8
NT = 48
NA = 6
T = 128

BAR, S1, S2, S3, P1, P2, X3, Y3, Y4, Q4, O4, O5, D5 = range(13)


def split(x):
    high = x.astype(BF16)
    return high, (x - high.astype(F32)).astype(BF16)


def dot3(a, b):
    ah, al = a
    bh, bl = b
    dot = lambda u, v: jnp.dot(u, v, preferred_element_type=F32)
    return dot(ah, bh) + (dot(ah, bl) + dot(al, bh))


def kernel(
    anc,
    sep,
    pan,
    off,
    quad,
    s_rows,
    s_by_tile,
    s_col,
    s_tiles,
    s_unit,
    s_fin,
    p_cols,
    p_perm,
    p_rows,
    p_unit,
    x_buf,
    y_units,
    y_buf,
    y_hi,
    y_lo,
    q_unit,
    q_buf,
    off_st,
    off_cols,
    d_st,
    send,
    recv,
):
    r = lax.axis_index("row")
    c = lax.axis_index("col")
    s = lax.div(r, HALF)
    b = lax.rem(r, HALF)

    def remote(src, dst, i, device):
        return pltpu.make_async_remote_copy(
            src_ref=src,
            dst_ref=dst,
            send_sem=send.at[i],
            recv_sem=recv.at[i],
            device_id=device,
            device_id_type=MESH,
        )

    def local(src, dst, i):
        return pltpu.make_async_copy(src, dst, recv.at[i])

    def push(src, dst, i, dr, dc):
        here = jnp.logical_and(dr == r, dc == c)

        @pl.when(here)
        def _():
            local(src, dst, i).start()

        @pl.when(jnp.logical_not(here))
        def _():
            remote(src, dst, i, (dr, dc)).start()

    def take(sem, ref):
        pltpu.make_async_copy(ref, ref, sem).wait()

    def loop(lo, hi, body):
        def step(i, carry):
            body(i)
            return carry

        lax.fori_loop(lo, hi, step, 0)

    barrier = pltpu.get_barrier_semaphore()

    def greet(i):
        for device in ((lax.rem(r + i, N), c), (r, lax.rem(c + i, N))):
            pl.semaphore_signal(barrier, inc=1, device_id=device, device_id_type=MESH)

    loop(1, N, greet)
    pl.semaphore_wait(barrier, 2 * (N - 1))

    def send_s(i):
        d = lax.rem(c + i, N)
        remote(sep.at[:, pl.ds(8 * d, 8), :], s_rows.at[c], S1, (r, d)).start()

    loop(1, N, send_s)
    local(sep.at[:, pl.ds(8 * c, 8), :], s_rows.at[c], S1).start()

    def columns(d):
        return pan.at[:, :, pl.ds(pl.multiple_of(T * d, T), T)]

    def send_p(i):
        d = lax.rem(r + i, N)
        remote(columns(d), p_cols.at[r], P1, (d, c)).start()

    loop(1, N, send_p)
    local(columns(r), p_cols.at[r], P1).start()

    take(recv.at[P1], p_cols)

    def send_p2(q):
        piece = 3 * c + q
        push(p_cols.at[:, q], p_perm.at[lax.div(piece, N)], P2, r, lax.rem(piece, N))

    loop(0, 3, send_p2)

    take(recv.at[S1], s_rows)
    for j in range(N):
        for v in range(3):
            s_by_tile[3 * j + v] = s_rows[j, :, :, T * v : T * v + T]
    for t in range(2):
        for l in range(NA):
            s_col[t, l] = s_by_tile[anc[t, l]]

    def send_s2(i):
        t = lax.div(i, NA)
        l = lax.rem(i, NA)
        push(s_col.at[t, l], s_tiles.at[pl.ds(3 * r, 3)], S2, HALF * t + l, c)

    loop(0, 2 * NA, send_s2)

    take(recv.at[P2], p_perm)
    for j in range(N):
        for m in range(3):
            p_rows[3 * j + m] = p_perm[m, j]
    for k in range(NA):
        p_unit[k] = p_rows[anc[s, k]]

    def send_x(i):
        d = lax.rem(c + i, N)
        remote(p_unit, x_buf.at[:, c], X3, (r, d)).start()

    loop(1, N, send_x)
    x_buf[:, pl.ds(c, 1)] = p_unit[...][:, None]

    def send_y(i):
        d = HALF * s + lax.rem(b + i, HALF)
        remote(p_unit, y_units.at[b], Y3, (d, c)).start()

    loop(1, HALF, send_y)
    local(p_unit, y_units.at[b], Y3).start()

    @pl.when(b < NA)
    def _():
        take(recv.at[S2], s_tiles)
        for k in range(NA):
            s_unit[k] = s_tiles[anc[s, k]]

        def send_s3(i):
            d = HALF * s + lax.rem(b + i, HALF)
            remote(s_unit, s_fin.at[b], S3, (d, c)).start()

        loop(1, HALF, send_s3)
        local(s_unit, s_fin.at[b], S3).start()

    take(recv.at[Y3], y_units)

    def send_y4(i):
        d = lax.rem(c + i, N)
        remote(y_units.at[lax.div(d, 2)], y_buf.at[:, c], Y4, (r, d)).start()

    loop(1, N, send_y4)
    local(y_units.at[lax.div(c, 2)], y_buf.at[:, c], Y4).start()

    take(recv.at[X3], x_buf.at[:, pl.ds(0, N - 1)])
    take(recv.at[S3], s_fin)
    acc = jnp.zeros((NA * 8, T), F32)
    for l in range(NA):
        acc += dot3(split(s_fin[l].reshape(NA * 8, T)), split(x_buf[l].reshape(T, T)))
    q_unit[pl.ds(0, NA)] = acc.reshape(NA, 8, T)
    q_unit[NA] = jnp.zeros((8, T), F32)

    def send_q(i):
        d = lax.rem(c + i, N)
        remote(q_unit.at[pl.ds(0, NA)], q_buf.at[:, c], Q4, (r, d)).start()

    loop(1, N, send_q)
    q_buf[:, pl.ds(c, 1)] = q_unit[pl.ds(0, NA)][:, None]

    for t in range(NT):
        place = NA
        for k in range(NA):
            place = jnp.minimum(place, NA - (anc[s, k] == t).astype(jnp.int32) * (NA - k))
        off_st[t] = -q_unit[place]

    def send_off(i):
        d = lax.rem(r + i, N)
        remote(off_st.at[pl.ds(3 * d, 3)], off_cols.at[r], O4, (d, c)).start()

    loop(1, N, send_off)
    local(off_st.at[pl.ds(3 * r, 3)], off_cols.at[r], O4).start()

    take(recv.at[Y4], y_buf)
    for k in range(NA):
        hi, lo = split(y_buf[k].reshape(T, T).T)
        y_hi[k] = hi
        y_lo[k] = lo

    take(recv.at[Q4], q_buf.at[:, pl.ds(0, N - 1)])
    rows = pl.ds(pl.multiple_of(lax.rem(c, 2) * 64, 64), 64)
    acc = jnp.zeros((64, T), F32)
    for k in range(NA):
        acc += dot3((y_hi[k, rows, :], y_lo[k, rows, :]), split(q_buf[k].reshape(T, T)))
    d_st[...] = acc.reshape(N, 4, T)

    def send_d(i):
        d = lax.rem(c + i, N)
        push(d_st.at[d], quad.at[r], D5, c, d)

    loop(0, N, send_d)

    take(recv.at[O4], off_cols)

    def send_off2(m):
        piece = N * m + c
        push(off_cols.at[:, m], off.at[lax.rem(piece, 3)], O5, r, lax.div(piece, 3))

    loop(0, 3, send_off2)

    take(send.at[S1], s_rows.at[pl.ds(0, N - 1)])
    take(send.at[P1], p_cols.at[pl.ds(0, N - 1)])
    take(send.at[X3], x_buf.at[:, pl.ds(0, N - 1)])
    take(send.at[Y3], y_units.at[pl.ds(0, HALF - 1)])
    take(send.at[Y4], y_buf.at[:, pl.ds(0, N - 1)])
    take(send.at[Q4], q_buf.at[:, pl.ds(0, N - 1)])
    take(send.at[O4], off_cols.at[pl.ds(0, N - 1)])

    @pl.when(b < NA)
    def _():
        take(send.at[S3], s_tiles.at[pl.ds(0, 7 * NA)])
        take(send.at[S2], s_tiles.at[pl.ds(0, 33)])

    @pl.when(b >= NA)
    def _():
        take(send.at[S2], s_tiles.at[pl.ds(0, 36)])

    own = jnp.logical_or(jnp.logical_or(c == 0, c == 7), jnp.logical_or(c == 8, c == 15))

    @pl.when(own)
    def _():
        take(send.at[P2], p_perm.at[pl.ds(0, 2)])
        take(send.at[O5], p_perm.at[pl.ds(0, 2)])

    @pl.when(jnp.logical_not(own))
    def _():
        take(send.at[P2], p_perm)
        take(send.at[O5], p_perm)

    @pl.when(r == c)
    def _():
        take(send.at[D5], d_st.at[pl.ds(0, N - 1)])

    @pl.when(r != c)
    def _():
        take(send.at[D5], d_st)

    take(recv.at[O5], off)
    take(recv.at[D5], quad)


def per_device(separator_inverse, panels, diag_inverse, ancestors):
    hbm = pl.BlockSpec(memory_space=pl.ANY)
    vmem = pltpu.VMEM
    off, quad = pl.pallas_call(
        kernel,
        out_shape=(
            jax.ShapeDtypeStruct((3, N, 8, T), F32),
            jax.ShapeDtypeStruct((N, 4, T), F32),
        ),
        in_specs=[pl.BlockSpec(memory_space=pltpu.SMEM), hbm, hbm],
        out_specs=(hbm, pl.BlockSpec(memory_space=pltpu.VMEM)),
        scratch_shapes=[
            vmem((N, 3, 8, 3 * T), F32),
            vmem((NT, 3, 8, T), F32),
            vmem((2, NA, 3, 8, T), F32),
            vmem((NT, 8, T), F32),
            vmem((NA, 8, T), F32),
            vmem((NA, NA, 8, T), F32),
            vmem((N, 3, 8, T), F32),
            vmem((3, N, 8, T), F32),
            vmem((NT, 8, T), F32),
            vmem((NA, 8, T), F32),
            vmem((NA, N, 8, T), F32),
            vmem((HALF, NA, 8, T), F32),
            vmem((NA, N, 8, T), F32),
            vmem((NA, T, T), BF16),
            vmem((NA, T, T), BF16),
            vmem((NA + 1, 8, T), F32),
            vmem((NA, N, 8, T), F32),
            vmem((NT, 8, T), F32),
            vmem((N, 3, 8, T), F32),
            vmem((N, 4, T), F32),
            pltpu.SemaphoreType.DMA((13,)),
            pltpu.SemaphoreType.DMA((13,)),
        ],
        compiler_params=pltpu.CompilerParams(collective_id=0, has_side_effects=True),
        name="selected_inverse",
    )(
        ancestors,
        separator_inverse.reshape(3, T, 3 * T),
        panels.reshape(3, 8, 2 * HALF * T),
    )
    quad_rows = quad.reshape(2, HALF, 4, T).transpose(0, 2, 1, 3).reshape(2, 4, HALF * T)
    off_rows = off.transpose(0, 2, 1, 3).reshape(24, 2 * HALF * T)
    return off_rows, diag_inverse + quad_rows


def solution(mesh):
    return jax.shard_map(
        per_device,
        mesh=mesh,
        in_specs=(P("row", "col"), P(("row", "col"), None), P(None, ("row", "col"), None), P()),
        out_specs=(P(("row", "col"), None), P(None, ("row", "col"), None)),
        check_vma=False,
    )
```

```python
import jax
import jax.numpy as jnp
from jax import lax
from jax.experimental import pallas as pl
from jax.experimental.pallas import tpu as pltpu
from jax.sharding import PartitionSpec as P

MESH = pl.DeviceIdType.MESH
F32 = jnp.float32
BF16 = jnp.bfloat16
N = 16
HALF = 8
NT = 48
NA = 6
T = 128

S1, S2, S3, P1, P2, X3, Y4, Q4, O5, D5 = range(10)


def split(x):
    high = x.astype(BF16)
    return high, (x - high.astype(F32)).astype(BF16)


def dot3(a, b):
    ah, al = a
    bh, bl = b
    dot = lambda u, v: jnp.dot(u, v, preferred_element_type=F32)
    return dot(ah, bh) + (dot(ah, bl) + dot(al, bh))


def kernel(
    anc,
    sep,
    pan,
    off,
    quad,
    place,
    s_rows,
    s_by_tile,
    s_col,
    s_tiles,
    s_unit,
    s_fin,
    p_cols,
    p_send,
    p_perm,
    p_unit,
    x_buf,
    x_t,
    y_unit,
    y_buf,
    q_unit,
    q_buf,
    off_st,
    d_st,
    send,
    recv,
):
    r = lax.axis_index("row")
    c = lax.axis_index("col")
    s = lax.div(r, HALF)
    b = lax.rem(r, HALF)

    def remote(src, dst, i, device):
        return pltpu.make_async_remote_copy(
            src_ref=src,
            dst_ref=dst,
            send_sem=send.at[i],
            recv_sem=recv.at[i],
            device_id=device,
            device_id_type=MESH,
        )

    def local(src, dst, i):
        return pltpu.make_async_copy(src, dst, recv.at[i])

    def push(src, dst, i, dr, dc):
        here = jnp.logical_and(dr == r, dc == c)

        @pl.when(here)
        def _():
            local(src, dst, i).start()

        @pl.when(jnp.logical_not(here))
        def _():
            remote(src, dst, i, (dr, dc)).start()

    def take(sem, ref):
        pltpu.make_async_copy(ref, ref, sem).wait()

    def loop(lo, hi, body):
        def step(i, carry):
            body(i)
            return carry

        lax.fori_loop(lo, hi, step, 0)

    def over_col(i):
        j = N - 1 - i
        half, along, core = lax.div(j, 8), lax.rem(lax.div(j, 2), 4), lax.rem(j, 2)
        along = lax.div(along * (along + 1), 2)
        return (
            8 * lax.rem(lax.div(c, 8) + half, 2)
            + 2 * lax.rem(lax.div(c, 2) + along, 4)
            + lax.rem(c + core, 2)
        )

    def over_row(i):
        j = lax.div(i, 2)
        z = 4 + (1 - 2 * lax.rem(j, 2)) * lax.div(j + 1, 2)
        return 2 * lax.rem(lax.div(r, 2) + z, HALF) + lax.rem(r + 1 + i, 2)

    def over_half(i):
        j = 3 - lax.div(i, 2)
        z = lax.div(j * (j + 1), 2)
        return HALF * s + 2 * lax.rem(lax.div(b, 2) + z, 4) + lax.rem(b + 1 + i, 2)

    barrier = pltpu.get_barrier_semaphore()

    def greet(i):
        for device in ((over_row(i), c), (r, over_col(i))):
            pl.semaphore_signal(barrier, inc=1, device_id=device, device_id_type=MESH)

    loop(0, N - 1, greet)
    pl.semaphore_wait(barrier, 2 * (N - 1))

    def send_s(i):
        d = over_col(i)
        remote(sep.at[:, pl.ds(8 * d, 8), :], s_rows.at[c], S1, (r, d)).start()

    loop(0, N - 1, send_s)
    local(sep.at[:, pl.ds(8 * c, 8), :], s_rows.at[c], S1).start()

    def columns(d):
        return pan.at[:, :, pl.ds(pl.multiple_of(T * d, T), T)]

    def send_p(i):
        d = over_row(i)
        remote(columns(d), p_cols.at[r], P1, (d, c)).start()

    loop(0, N - 1, send_p)
    local(columns(r), p_cols.at[r], P1).start()

    row_of = []
    for k in range(NA):
        value = 0
        for j in range(1, N):
            value += (anc[s, k] >= 3 * j).astype(jnp.int32)
        row_of.append(value)
    for t in range(NT):
        value = NA
        for k in range(NA):
            value = jnp.minimum(value, NA - (anc[s, k] == t).astype(jnp.int32) * (NA - k))
        place[t] = value

    take(recv.at[P1], p_cols)
    for k in range(NA):
        for q in range(3):
            p_send[q, k] = p_cols[row_of[k], q]

    def send_p2(q):
        piece = 3 * c + q
        push(p_send.at[q], p_perm.at[lax.div(piece, N)], P2, r, lax.rem(piece, N))

    loop(0, 3, send_p2)

    take(recv.at[S1], s_rows)
    for j in range(N):
        for v in range(3):
            s_by_tile[3 * j + v] = s_rows[j, :, :, T * v : T * v + T]
    for t in range(2):
        for l in range(NA):
            s_col[t, l] = s_by_tile[anc[t, l]]

    def send_s2(i):
        d = over_row(i)
        l = lax.rem(d, HALF)

        @pl.when(l < NA)
        def _():
            src = s_col.at[lax.div(d, HALF), l]
            remote(src, s_tiles.at[pl.ds(3 * r, 3)], S2, (d, c)).start()

    loop(0, N - 1, send_s2)

    @pl.when(b < NA)
    def _():
        local(s_col.at[s, b], s_tiles.at[pl.ds(3 * r, 3)], S2).start()

    take(recv.at[P2], p_perm)
    for k in range(NA):
        p_unit[k] = p_perm[anc[s, k] - 3 * row_of[k], k]

    def send_x(i):
        d = over_col(i)
        remote(p_unit, x_buf.at[:, c], X3, (r, d)).start()

    loop(0, N - 1, send_x)
    x_buf[:, pl.ds(c, 1)] = p_unit[...][:, None]

    @pl.when(b < NA)
    def _():
        take(recv.at[S2], s_tiles)
        for k in range(NA):
            s_unit[k] = s_tiles[anc[s, k]]

        def send_s3(i):
            d = over_half(i)
            remote(s_unit, s_fin.at[b], S3, (d, c)).start()

        loop(0, HALF - 1, send_s3)
        local(s_unit, s_fin.at[b], S3).start()

    take(recv.at[X3], x_buf.at[:, pl.ds(0, N - 1)])
    for k in range(NA):
        x_t[:, :, T * k : T * (k + 1)] = x_buf[k].reshape(T, T).T.reshape(2 * N, 4, T)
    y_unit[0:4] = x_t[c]
    y_unit[4:8] = x_t[N + c]

    def send_y4(i):
        d = over_half(i)
        remote(y_unit, y_buf.at[b], Y4, (d, c)).start()

    loop(0, HALF - 1, send_y4)
    local(y_unit, y_buf.at[b], Y4).start()

    take(recv.at[S3], s_fin)
    acc = jnp.zeros((NA * 8, T), F32)
    for l in range(NA):
        acc += dot3(split(s_fin[l].reshape(NA * 8, T)), split(x_buf[l].reshape(T, T)))
    q_unit[...] = acc.reshape(NA, 8, T)

    def send_q(i):
        d = over_col(i)
        remote(q_unit, q_buf.at[pl.ds(0, NA), c], Q4, (r, d)).start()

    loop(0, N - 1, send_q)
    q_buf[0:NA, pl.ds(c, 1)] = q_unit[...][:, None]
    q_buf[NA] = jnp.zeros((N, 8, T), F32)

    take(recv.at[Y4], y_buf)
    y_halves = split(y_buf[...].reshape(HALF * 8, NA * T))
    take(recv.at[Q4], q_buf.at[pl.ds(0, NA), pl.ds(0, N - 1)])

    for q in range(3):
        piece = 3 * c + q
        m, o = lax.div(piece, N), lax.rem(piece, N)
        for j in range(N):
            off_st[j, q] = -q_buf[place[3 * j + m], o]

    def send_off(i):
        d = over_row(i)
        remote(off_st.at[d], off.at[:, r], O5, (d, c)).start()

    loop(0, N - 1, send_off)
    local(off_st.at[r], off.at[:, r], O5).start()

    acc = dot3(y_halves, split(q_buf[0:NA].reshape(NA * T, T)))
    d_st[...] = acc.reshape(N, 4, T)

    def send_d(i):
        d = over_row(i)
        remote(d_st.at[d], quad.at[r], D5, (d, c)).start()

    loop(0, N - 1, send_d)
    local(d_st.at[r], quad.at[r], D5).start()

    take(send.at[S1], s_rows.at[pl.ds(0, N - 1)])
    take(send.at[P1], p_cols.at[pl.ds(0, N - 1)])
    take(send.at[X3], x_buf.at[:, pl.ds(0, N - 1)])
    take(send.at[Y4], y_buf.at[pl.ds(0, HALF - 1)])
    take(send.at[Q4], x_buf.at[:, pl.ds(0, N - 1)])
    take(send.at[O5], off_st.at[pl.ds(0, N - 1)])
    take(send.at[D5], d_st.at[pl.ds(0, N - 1)])

    @pl.when(b < NA)
    def _():
        take(send.at[S3], s_tiles.at[pl.ds(0, 7 * NA)])
        take(send.at[S2], s_tiles.at[pl.ds(0, 33)])

    @pl.when(b >= NA)
    def _():
        take(send.at[S2], s_tiles.at[pl.ds(0, 36)])

    own = jnp.logical_or(jnp.logical_or(c == 0, c == 7), jnp.logical_or(c == 8, c == 15))

    @pl.when(own)
    def _():
        take(send.at[P2], p_perm.at[pl.ds(0, 2)])

    @pl.when(jnp.logical_not(own))
    def _():
        take(send.at[P2], p_perm)

    take(recv.at[O5], off)
    take(recv.at[D5], quad)


def per_device(separator_inverse, panels, diag_inverse, ancestors):
    hbm = pl.BlockSpec(memory_space=pl.ANY)
    vmem = pltpu.VMEM
    off, quad = pl.pallas_call(
        kernel,
        out_shape=(
            jax.ShapeDtypeStruct((3, N, 8, T), F32),
            jax.ShapeDtypeStruct((N, 4, T), F32),
        ),
        in_specs=[pl.BlockSpec(memory_space=pltpu.SMEM), hbm, hbm],
        out_specs=(hbm, pl.BlockSpec(memory_space=pltpu.VMEM)),
        scratch_shapes=[
            pltpu.SMEM((NT,), jnp.int32),
            vmem((N, 3, 8, 3 * T), F32),
            vmem((NT, 3, 8, T), F32),
            vmem((2, NA, 3, 8, T), F32),
            vmem((NT, 8, T), F32),
            vmem((NA, 8, T), F32),
            vmem((NA, NA, 8, T), F32),
            vmem((N, 3, 8, T), F32),
            vmem((3, NA, 8, T), F32),
            vmem((3, NA, 8, T), F32),
            vmem((NA, 8, T), F32),
            vmem((NA, N, 8, T), F32),
            vmem((2 * N, 4, NA * T), F32),
            vmem((8, NA * T), F32),
            vmem((HALF, 8, NA * T), F32),
            vmem((NA, 8, T), F32),
            vmem((NA + 1, N, 8, T), F32),
            vmem((N, 3, 8, T), F32),
            vmem((N, 4, T), F32),
            pltpu.SemaphoreType.DMA((10,)),
            pltpu.SemaphoreType.DMA((10,)),
        ],
        compiler_params=pltpu.CompilerParams(collective_id=0, has_side_effects=True),
        name="selected_inverse",
    )(
        ancestors,
        separator_inverse.reshape(3, T, 3 * T),
        panels.reshape(3, 8, 2 * HALF * T),
    )
    quad_rows = quad.reshape(2, HALF, 4, T).transpose(0, 2, 1, 3).reshape(2, 4, HALF * T)
    off_rows = off.transpose(0, 2, 1, 3).reshape(24, 2 * HALF * T)
    return off_rows, diag_inverse + quad_rows


def solution(mesh):
    return jax.shard_map(
        per_device,
        mesh=mesh,
        in_specs=(P("row", "col"), P(("row", "col"), None), P(None, ("row", "col"), None), P()),
        out_specs=(P(("row", "col"), None), P(None, ("row", "col"), None)),
        check_vma=False,
    )
```

```python
import jax
import jax.numpy as jnp
from jax import lax
from jax.experimental import pallas as pl
from jax.experimental.pallas import tpu as pltpu
from jax.sharding import PartitionSpec as P

MESH = pl.DeviceIdType.MESH
F32 = jnp.float32
BF16 = jnp.bfloat16
N = 16
HALF = 8
NT = 48
NA = 6
T = 128

S2, S3, P1, P2, X3, Y4, Q4, O4, O5, D5, S1 = range(11)


def split(x):
    high = x.astype(BF16)
    return high, (x - high.astype(F32)).astype(BF16)


def dot3(a, b):
    ah, al = a
    bh, bl = b
    dot = lambda u, v: jnp.dot(u, v, preferred_element_type=F32)
    return dot(ah, bh) + (dot(ah, bl) + dot(al, bh))


def kernel(
    anc,
    sep,
    pan,
    off,
    quad,
    place,
    s_rows,
    s_by_tile,
    s_col,
    s_tiles,
    s_unit,
    s_fin,
    p_cols,
    p_send,
    p_perm,
    p_unit,
    x_buf,
    x_t,
    y_unit,
    y_buf,
    q_unit,
    q_buf,
    off_st,
    off_cols,
    d_st,
    send,
    recv,
):
    r = lax.axis_index("row")
    c = lax.axis_index("col")
    s = lax.div(r, HALF)
    b = lax.rem(r, HALF)

    def remote(src, dst, i, device):
        return pltpu.make_async_remote_copy(
            src_ref=src,
            dst_ref=dst,
            send_sem=send.at[i],
            recv_sem=recv.at[i],
            device_id=device,
            device_id_type=MESH,
        )

    def local(src, dst, i):
        return pltpu.make_async_copy(src, dst, recv.at[i])

    def push(src, dst, i, dr, dc):
        here = jnp.logical_and(dr == r, dc == c)

        @pl.when(here)
        def _():
            local(src, dst, i).start()

        @pl.when(jnp.logical_not(here))
        def _():
            remote(src, dst, i, (dr, dc)).start()

    def take(sem, ref):
        pltpu.make_async_copy(ref, ref, sem).wait()

    def loop(lo, hi, body):
        def step(i, carry):
            body(i)
            return carry

        lax.fori_loop(lo, hi, step, 0)

    def over_col(i):
        j = N - 1 - i
        half, along, core = lax.div(j, 8), lax.rem(lax.div(j, 2), 4), lax.rem(j, 2)
        along = lax.div(along * (along + 1), 2)
        return (
            8 * lax.rem(lax.div(c, 8) + half, 2)
            + 2 * lax.rem(lax.div(c, 2) + along, 4)
            + lax.rem(c + core, 2)
        )

    def over_row(i):
        j = lax.div(i, 2)
        z = 4 + (1 - 2 * lax.rem(j, 2)) * lax.div(j + 1, 2)
        return 2 * lax.rem(lax.div(r, 2) + z, HALF) + lax.rem(r + 1 + i, 2)

    def over_half(i):
        j = 3 - lax.div(i, 2)
        z = lax.div(j * (j + 1), 2)
        return HALF * s + 2 * lax.rem(lax.div(b, 2) + z, 4) + lax.rem(b + 1 + i, 2)

    barrier = pltpu.get_barrier_semaphore()

    def greet(i):
        for device in ((over_row(i), c), (r, over_col(i))):
            pl.semaphore_signal(barrier, inc=1, device_id=device, device_id_type=MESH)

    loop(0, N - 1, greet)
    pl.semaphore_wait(barrier, 2 * (N - 1))

    for m in range(3):

        def send_s(i, m=m):
            d = over_col(i)
            remote(sep.at[m, pl.ds(8 * d, 8), :], s_rows.at[m, c], S1 + m, (r, d)).start()

        loop(0, N - 1, send_s)
        local(sep.at[m, pl.ds(8 * c, 8), :], s_rows.at[m, c], S1 + m).start()

    def columns(d):
        return pan.at[:, :, pl.ds(pl.multiple_of(T * d, T), T)]

    def send_p(i):
        d = over_row(i)
        remote(columns(d), p_cols.at[r], P1, (d, c)).start()

    loop(0, N - 1, send_p)
    local(columns(r), p_cols.at[r], P1).start()

    row_of = []
    for k in range(NA):
        value = 0
        for j in range(1, N):
            value += (anc[s, k] >= 3 * j).astype(jnp.int32)
        row_of.append(value)
    for t in range(NT):
        value = NA
        for k in range(NA):
            value = jnp.minimum(value, NA - (anc[s, k] == t).astype(jnp.int32) * (NA - k))
        place[t] = value

    take(recv.at[P1], p_cols)
    for k in range(NA):
        for q in range(3):
            p_send[q, k] = p_cols[row_of[k], q]

    def send_p2(q):
        piece = 3 * c + q
        push(p_send.at[q], p_perm.at[lax.div(piece, N)], P2, r, lax.rem(piece, N))

    loop(0, 3, send_p2)

    for m in range(3):
        take(recv.at[S1 + m], s_rows.at[m])
        for j in range(N):
            for v in range(3):
                s_by_tile[m, 3 * j + v] = s_rows[m, j, :, T * v : T * v + T]
        for t in range(2):
            for l in range(NA):
                s_col[m, t, l] = s_by_tile[m, anc[t, l]]

        def send_s2(i, m=m):
            d = over_row(i)
            l = lax.rem(d, HALF)

            @pl.when(l < NA)
            def _():
                src = s_col.at[m, lax.div(d, HALF), l]
                remote(src, s_tiles.at[3 * r + m], S2, (d, c)).start()

        loop(0, N - 1, send_s2)

        @pl.when(b < NA)
        def _():
            local(s_col.at[m, s, b], s_tiles.at[3 * r + m], S2).start()

    take(recv.at[P2], p_perm)
    for k in range(NA):
        p_unit[k] = p_perm[anc[s, k] - 3 * row_of[k], k]

    def send_x(i):
        d = over_col(i)
        remote(p_unit, x_buf.at[:, c], X3, (r, d)).start()

    loop(0, N - 1, send_x)
    x_buf[:, pl.ds(c, 1)] = p_unit[...][:, None]

    @pl.when(b < NA)
    def _():
        take(recv.at[S2], s_tiles)
        for k in range(NA):
            s_unit[k] = s_tiles[anc[s, k]]

        def send_s3(i):
            d = over_half(i)
            remote(s_unit, s_fin.at[b], S3, (d, c)).start()

        loop(0, HALF - 1, send_s3)
        local(s_unit, s_fin.at[b], S3).start()

    take(recv.at[X3], x_buf.at[:, pl.ds(0, N - 1)])
    for k in range(NA):
        x_t[:, :, T * k : T * (k + 1)] = x_buf[k].reshape(T, T).T.reshape(2 * N, 4, T)
    y_unit[0:4] = x_t[c]
    y_unit[4:8] = x_t[N + c]

    def send_y4(i):
        d = over_half(i)
        remote(y_unit, y_buf.at[b], Y4, (d, c)).start()

    loop(0, HALF - 1, send_y4)
    local(y_unit, y_buf.at[b], Y4).start()

    take(recv.at[S3], s_fin)
    acc = jnp.zeros((NA * 8, T), F32)
    for l in range(NA):
        acc += dot3(split(s_fin[l].reshape(NA * 8, T)), split(x_buf[l].reshape(T, T)))
    q_unit[0:NA] = acc.reshape(NA, 8, T)
    q_unit[NA] = jnp.zeros((8, T), F32)

    def send_q(i):
        d = over_col(i)
        remote(q_unit.at[pl.ds(0, NA)], q_buf.at[:, c], Q4, (r, d)).start()

    loop(0, N - 1, send_q)
    q_buf[:, pl.ds(c, 1)] = q_unit[0:NA][:, None]

    for t in range(NT):
        off_st[t] = -q_unit[place[t]]

    def send_off(i):
        d = over_row(i)
        remote(off_st.at[pl.ds(3 * d, 3)], off_cols.at[r], O4, (d, c)).start()

    loop(0, N - 1, send_off)
    local(off_st.at[pl.ds(3 * r, 3)], off_cols.at[r], O4).start()

    take(recv.at[Y4], y_buf)
    y_halves = split(y_buf[...].reshape(HALF * 8, NA * T))
    take(recv.at[Q4], q_buf.at[:, pl.ds(0, N - 1)])

    acc = dot3(y_halves, split(q_buf[...].reshape(NA * T, T)))
    d_st[...] = acc.reshape(N, 4, T)

    def send_d(i):
        d = over_row(i)
        remote(d_st.at[d], quad.at[r], D5, (d, c)).start()

    loop(0, N - 1, send_d)
    local(d_st.at[r], quad.at[r], D5).start()

    take(recv.at[O4], off_cols)

    def send_off2(m):
        piece = N * m + c
        push(off_cols.at[:, m], off.at[lax.rem(piece, 3)], O5, r, lax.div(piece, 3))

    loop(0, 3, send_off2)

    for m in range(3):
        take(send.at[S1 + m], s_rows.at[m, pl.ds(0, N - 1)])
    take(send.at[P1], p_cols.at[pl.ds(0, N - 1)])
    take(send.at[X3], x_buf.at[:, pl.ds(0, N - 1)])
    take(send.at[Y4], y_buf.at[pl.ds(0, HALF - 1)])
    take(send.at[Q4], x_buf.at[:, pl.ds(0, N - 1)])
    take(send.at[O4], off_cols.at[pl.ds(0, N - 1)])
    take(send.at[D5], d_st.at[pl.ds(0, N - 1)])

    @pl.when(b < NA)
    def _():
        take(send.at[S3], s_tiles.at[pl.ds(0, 7 * NA)])
        take(send.at[S2], s_tiles.at[pl.ds(0, 33)])

    @pl.when(b >= NA)
    def _():
        take(send.at[S2], s_tiles.at[pl.ds(0, 36)])

    own = jnp.logical_or(jnp.logical_or(c == 0, c == 7), jnp.logical_or(c == 8, c == 15))

    @pl.when(own)
    def _():
        take(send.at[P2], p_perm.at[pl.ds(0, 2)])
        take(send.at[O5], off_st.at[pl.ds(0, 2 * N)])

    @pl.when(jnp.logical_not(own))
    def _():
        take(send.at[P2], p_perm)
        take(send.at[O5], off_st)

    take(recv.at[O5], off)
    take(recv.at[D5], quad)


def finish(off, quad, diag, off_out, diag_out):
    off_out[...] = off[...]
    diag_out[...] = diag[...] + quad[...]


def per_device(separator_inverse, panels, diag_inverse, ancestors):
    hbm = pl.BlockSpec(memory_space=pl.ANY)
    vmem = pltpu.VMEM
    off, quad = pl.pallas_call(
        kernel,
        out_shape=(
            jax.ShapeDtypeStruct((3, N, 8, T), F32),
            jax.ShapeDtypeStruct((N, 4, T), F32),
        ),
        in_specs=[pl.BlockSpec(memory_space=pltpu.SMEM), hbm, hbm],
        out_specs=(hbm, pl.BlockSpec(memory_space=pltpu.VMEM)),
        scratch_shapes=[
            pltpu.SMEM((NT,), jnp.int32),
            vmem((3, N, 8, 3 * T), F32),
            vmem((3, NT, 8, T), F32),
            vmem((3, 2, NA, 8, T), F32),
            vmem((NT, 8, T), F32),
            vmem((NA, 8, T), F32),
            vmem((NA, NA, 8, T), F32),
            vmem((N, 3, 8, T), F32),
            vmem((3, NA, 8, T), F32),
            vmem((3, NA, 8, T), F32),
            vmem((NA, 8, T), F32),
            vmem((NA, N, 8, T), F32),
            vmem((2 * N, 4, NA * T), F32),
            vmem((8, NA * T), F32),
            vmem((HALF, 8, NA * T), F32),
            vmem((NA + 1, 8, T), F32),
            vmem((NA, N, 8, T), F32),
            vmem((NT, 8, T), F32),
            vmem((N, 3, 8, T), F32),
            vmem((N, 4, T), F32),
            pltpu.SemaphoreType.DMA((13,)),
            pltpu.SemaphoreType.DMA((13,)),
        ],
        compiler_params=pltpu.CompilerParams(collective_id=0, has_side_effects=True),
        name="selected_inverse",
    )(
        ancestors,
        separator_inverse.reshape(3, T, 3 * T),
        panels.reshape(3, 8, 2 * HALF * T),
    )
    diag = diag_inverse.reshape(2, 4, HALF, T).transpose(0, 2, 1, 3).reshape(N, 4, T)
    in_vmem = pl.BlockSpec(memory_space=pltpu.VMEM)
    off, diag = pl.pallas_call(
        finish,
        out_shape=(
            jax.ShapeDtypeStruct((3, N, 8, T), F32),
            jax.ShapeDtypeStruct((N, 4, T), F32),
        ),
        in_specs=[in_vmem, in_vmem, in_vmem],
        out_specs=(in_vmem, in_vmem),
        name="finish",
    )(off, quad, diag)
    diag = diag.reshape(2, HALF, 4, T).transpose(0, 2, 1, 3).reshape(2, 4, HALF * T)
    return off.transpose(0, 2, 1, 3).reshape(24, 2 * HALF * T), diag


def solution(mesh):
    return jax.shard_map(
        per_device,
        mesh=mesh,
        in_specs=(P("row", "col"), P(("row", "col"), None), P(None, ("row", "col"), None), P()),
        out_specs=(P(("row", "col"), None), P(None, ("row", "col"), None)),
        check_vma=False,
    )
```

```python
import jax
import jax.numpy as jnp
from jax import lax
from jax.experimental import pallas as pl
from jax.experimental.pallas import tpu as pltpu
from jax.sharding import PartitionSpec as P

MESH = pl.DeviceIdType.MESH
F32 = jnp.float32
BF16 = jnp.bfloat16
N = 16
HALF = 8
NT = 48
NA = 6
T = 128

X4, Q5, S2, S3, P1, P2, X3, Y4, Q4, O4, O5, D5, S1 = range(13)


def split(x):
    high = x.astype(BF16)
    return high, (x - high.astype(F32)).astype(BF16)


def dot3(a, b):
    ah, al = a
    bh, bl = b
    dot = lambda u, v: jnp.dot(u, v, preferred_element_type=F32)
    return dot(ah, bh) + (dot(ah, bl) + dot(al, bh))


def kernel(
    anc_hbm,
    sep_hbm,
    pan_hbm,
    off,
    quad,
    place,
    s_rows,
    s_by_tile,
    s_col,
    s_tiles,
    s_unit,
    s_fin,
    p_cols,
    p_send,
    p_perm,
    p_unit,
    x_buf,
    x_t,
    y_unit,
    y_buf,
    q_unit,
    q_buf,
    off_st,
    off_cols,
    d_st,
    anc,
    sep,
    pan,
    fetch,
    send,
    recv,
):
    r = lax.axis_index("row")
    c = lax.axis_index("col")
    s = lax.div(r, HALF)
    b = lax.rem(r, HALF)
    chip = lax.div(c, 2)
    core = lax.rem(c, 2)
    sibling = c + 1 - 2 * core

    def remote(src, dst, i, device):
        return pltpu.make_async_remote_copy(
            src_ref=src,
            dst_ref=dst,
            send_sem=send.at[i],
            recv_sem=recv.at[i],
            device_id=device,
            device_id_type=MESH,
        )

    def local(src, dst, i):
        return pltpu.make_async_copy(src, dst, recv.at[i])

    def push(src, dst, i, dr, dc):
        here = jnp.logical_and(dr == r, dc == c)

        @pl.when(here)
        def _():
            local(src, dst, i).start()

        @pl.when(jnp.logical_not(here))
        def _():
            remote(src, dst, i, (dr, dc)).start()

    def take(sem, ref):
        pltpu.make_async_copy(ref, ref, sem).wait()

    def loop(lo, hi, body):
        def step(i, carry):
            body(i)
            return carry

        lax.fori_loop(lo, hi, step, 0)

    def over_col(i):
        j = N - 1 - i
        half, along, core = lax.div(j, 8), lax.rem(lax.div(j, 2), 4), lax.rem(j, 2)
        along = lax.div(along * (along + 1), 2)
        return (
            8 * lax.rem(lax.div(c, 8) + half, 2)
            + 2 * lax.rem(lax.div(c, 2) + along, 4)
            + lax.rem(c + core, 2)
        )

    def over_chips(i):
        j = HALF - 1 - i
        half, along = lax.div(j, 4), lax.rem(j, 4)
        along = lax.div(along * (along + 1), 2)
        return 8 * lax.rem(lax.div(c, 8) + half, 2) + 2 * lax.rem(chip + along, 4) + core

    def over_row(i):
        j = lax.div(i, 2)
        z = 4 + (1 - 2 * lax.rem(j, 2)) * lax.div(j + 1, 2)
        return 2 * lax.rem(lax.div(r, 2) + z, HALF) + lax.rem(r + 1 + i, 2)

    def over_half(i):
        j = 3 - lax.div(i, 2)
        z = lax.div(j * (j + 1), 2)
        return HALF * s + 2 * lax.rem(lax.div(b, 2) + z, 4) + lax.rem(b + 1 + i, 2)

    barrier = pltpu.get_barrier_semaphore()

    def greet(i):
        for device in ((over_row(i), c), (r, over_col(i))):
            pl.semaphore_signal(barrier, inc=1, device_id=device, device_id_type=MESH)

    loop(0, N - 1, greet)
    for m in range(3):
        pltpu.make_async_copy(sep_hbm.at[m], sep.at[m], fetch.at[m]).start()
    pltpu.make_async_copy(pan_hbm, pan, fetch.at[3]).start()
    pltpu.make_async_copy(anc_hbm, anc, fetch.at[4]).start()
    for m in range(3):
        take(fetch.at[m], sep.at[m])
    take(fetch.at[3], pan)
    pltpu.make_async_copy(anc_hbm, anc, fetch.at[4]).wait()
    pl.semaphore_wait(barrier, 2 * (N - 1))

    for m in range(3):

        def send_s(i, m=m):
            d = over_col(i)
            remote(sep.at[m, pl.ds(8 * d, 8), :], s_rows.at[m, c], S1 + m, (r, d)).start()

        loop(0, N - 1, send_s)
        local(sep.at[m, pl.ds(8 * c, 8), :], s_rows.at[m, c], S1 + m).start()

    def columns(d):
        return pan.at[:, :, pl.ds(pl.multiple_of(T * d, T), T)]

    def send_p(i):
        d = over_row(i)
        remote(columns(d), p_cols.at[r], P1, (d, c)).start()

    loop(0, N - 1, send_p)
    local(columns(r), p_cols.at[r], P1).start()

    row_of = []
    for k in range(NA):
        value = 0
        for j in range(1, N):
            value += (anc[s, k] >= 3 * j).astype(jnp.int32)
        row_of.append(value)
    for t in range(NT):
        value = NA
        for k in range(NA):
            value = jnp.minimum(value, NA - (anc[s, k] == t).astype(jnp.int32) * (NA - k))
        place[t] = value

    take(recv.at[P1], p_cols)
    for k in range(NA):
        for q in range(3):
            p_send[q, k] = p_cols[row_of[k], q]

    def send_p2(q):
        piece = 3 * c + q
        push(p_send.at[q], p_perm.at[lax.div(piece, N)], P2, r, lax.rem(piece, N))

    loop(0, 3, send_p2)

    for m in range(3):
        take(recv.at[S1 + m], s_rows.at[m])
        for j in range(N):
            for v in range(3):
                s_by_tile[m, 3 * j + v] = s_rows[m, j, :, T * v : T * v + T]
        for t in range(2):
            for l in range(NA):
                s_col[m, t, l] = s_by_tile[m, anc[t, l]]

        def send_s2(i, m=m):
            d = over_row(i)
            l = lax.rem(d, HALF)

            @pl.when(l < NA)
            def _():
                src = s_col.at[m, lax.div(d, HALF), l]
                remote(src, s_tiles.at[3 * r + m], S2, (d, c)).start()

        loop(0, N - 1, send_s2)

        @pl.when(b < NA)
        def _():
            local(s_col.at[m, s, b], s_tiles.at[3 * r + m], S2).start()

    take(recv.at[P2], p_perm)
    for k in range(NA):
        p_unit[k] = p_perm[anc[s, k] - 3 * row_of[k], k]

    def send_x(i):
        d = over_chips(i)
        remote(p_unit, x_buf.at[:, chip, core], X3, (r, d)).start()

    loop(0, HALF - 1, send_x)
    x_buf[:, pl.ds(chip, 1), pl.ds(core, 1)] = p_unit[...][:, None, None]

    @pl.when(b < NA)
    def _():
        take(recv.at[S2], s_tiles)
        for k in range(NA):
            s_unit[k] = s_tiles[anc[s, k]]

        def send_s3(i):
            d = over_half(i)
            remote(s_unit, s_fin.at[b], S3, (d, c)).start()

        loop(0, HALF - 1, send_s3)
        local(s_unit, s_fin.at[b], S3).start()

    take(recv.at[X3], x_buf.at[:, pl.ds(0, HALF - 1), 0])
    remote(x_buf.at[:, :, core], x_buf.at[:, :, core], X4, (r, sibling)).start()
    take(recv.at[X4], x_buf.at[:, :, 0])
    for k in range(NA):
        x_t[:, :, T * k : T * (k + 1)] = x_buf[k].reshape(T, T).T.reshape(2 * N, 4, T)
    y_unit[0:4] = x_t[c]
    y_unit[4:8] = x_t[N + c]

    def send_y4(i):
        d = over_half(i)
        remote(y_unit, y_buf.at[b], Y4, (d, c)).start()

    loop(0, HALF - 1, send_y4)
    local(y_unit, y_buf.at[b], Y4).start()

    take(recv.at[S3], s_fin)
    acc = jnp.zeros((NA * 8, T), F32)
    for l in range(NA):
        acc += dot3(split(s_fin[l].reshape(NA * 8, T)), split(x_buf[l].reshape(T, T)))
    q_unit[0:NA] = acc.reshape(NA, 8, T)
    q_unit[NA] = jnp.zeros((8, T), F32)

    def send_q(i):
        d = over_col(i)
        remote(q_unit.at[pl.ds(0, NA)], q_buf.at[:, c], Q4, (r, d)).start()

    loop(0, N - 1, send_q)
    q_buf[:, pl.ds(c, 1)] = q_unit[0:NA][:, None]

    for t in range(NT):
        off_st[t] = -q_unit[place[t]]

    def send_off(i):
        d = over_row(i)
        remote(off_st.at[pl.ds(3 * d, 3)], off_cols.at[r], O4, (d, c)).start()

    loop(0, N - 1, send_off)
    local(off_st.at[pl.ds(3 * r, 3)], off_cols.at[r], O4).start()

    take(recv.at[Y4], y_buf)
    y_halves = split(y_buf[...].reshape(HALF * 8, NA * T))
    take(recv.at[Q4], q_buf.at[:, pl.ds(0, N - 1)])

    acc = dot3(y_halves, split(q_buf[...].reshape(NA * T, T)))
    d_st[...] = acc.reshape(N, 4, T)

    def send_d(i):
        d = over_row(i)
        remote(d_st.at[d], quad.at[r], D5, (d, c)).start()

    loop(0, N - 1, send_d)
    local(d_st.at[r], quad.at[r], D5).start()

    take(recv.at[O4], off_cols)

    def send_off2(m):
        piece = N * m + c
        push(off_cols.at[:, m], off.at[lax.rem(piece, 3)], O5, r, lax.div(piece, 3))

    loop(0, 3, send_off2)

    for m in range(3):
        take(send.at[S1 + m], s_rows.at[m, pl.ds(0, N - 1)])
    take(send.at[P1], p_cols.at[pl.ds(0, N - 1)])
    take(send.at[X3], x_buf.at[:, pl.ds(0, HALF - 1), 0])
    take(send.at[X4], x_buf.at[:, :, 0])
    take(send.at[Y4], y_buf.at[pl.ds(0, HALF - 1)])
    take(send.at[Q4], q_buf.at[:, pl.ds(0, N - 1)])
    take(send.at[O4], off_cols.at[pl.ds(0, N - 1)])
    take(send.at[D5], d_st.at[pl.ds(0, N - 1)])

    @pl.when(b < NA)
    def _():
        take(send.at[S3], s_tiles.at[pl.ds(0, 7 * NA)])
        take(send.at[S2], s_tiles.at[pl.ds(0, 33)])

    @pl.when(b >= NA)
    def _():
        take(send.at[S2], s_tiles.at[pl.ds(0, 36)])

    own = jnp.logical_or(jnp.logical_or(c == 0, c == 7), jnp.logical_or(c == 8, c == 15))

    @pl.when(own)
    def _():
        take(send.at[P2], p_perm.at[pl.ds(0, 2)])
        take(send.at[O5], off_st.at[pl.ds(0, 2 * N)])

    @pl.when(jnp.logical_not(own))
    def _():
        take(send.at[P2], p_perm)
        take(send.at[O5], off_st)

    take(recv.at[O5], off)
    take(recv.at[D5], quad)


def finish(off, quad, diag, off_out, diag_out):
    off_out[...] = off[...]
    diag_out[...] = diag[...] + quad[...]


def per_device(separator_inverse, panels, diag_inverse, ancestors):
    hbm = pl.BlockSpec(memory_space=pl.ANY)
    vmem = pltpu.VMEM
    off, quad = pl.pallas_call(
        kernel,
        out_shape=(
            jax.ShapeDtypeStruct((3, N, 8, T), F32),
            jax.ShapeDtypeStruct((N, 4, T), F32),
        ),
        in_specs=[hbm, hbm, hbm],
        out_specs=(hbm, hbm),
        scratch_shapes=[
            pltpu.SMEM((NT,), jnp.int32),
            vmem((3, N, 8, 3 * T), F32),
            vmem((3, NT, 8, T), F32),
            vmem((3, 2, NA, 8, T), F32),
            vmem((NT, 8, T), F32),
            vmem((NA, 8, T), F32),
            vmem((NA, NA, 8, T), F32),
            vmem((N, 3, 8, T), F32),
            vmem((3, NA, 8, T), F32),
            vmem((3, NA, 8, T), F32),
            vmem((NA, 8, T), F32),
            vmem((NA, HALF, 2, 8, T), F32),
            vmem((2 * N, 4, NA * T), F32),
            vmem((8, NA * T), F32),
            vmem((HALF, 8, NA * T), F32),
            vmem((NA + 1, 8, T), F32),
            vmem((NA, N, 8, T), F32),
            vmem((NT, 8, T), F32),
            vmem((N, 3, 8, T), F32),
            vmem((N, 4, T), F32),
            pltpu.SMEM((2, NA), jnp.int32),
            vmem((3, T, 3 * T), F32),
            vmem((3, 8, 2 * HALF * T), F32),
            pltpu.SemaphoreType.DMA((5,)),
            pltpu.SemaphoreType.DMA((15,)),
            pltpu.SemaphoreType.DMA((15,)),
        ],
        compiler_params=pltpu.CompilerParams(collective_id=0, has_side_effects=True),
        name="selected_inverse",
    )(
        ancestors,
        separator_inverse.reshape(3, T, 3 * T),
        panels.reshape(3, 8, 2 * HALF * T),
    )
    diag = diag_inverse.reshape(2, 4, HALF, T).transpose(0, 2, 1, 3).reshape(N, 4, T)
    in_vmem = pl.BlockSpec(memory_space=pltpu.VMEM)
    off, diag = pl.pallas_call(
        finish,
        out_shape=(
            jax.ShapeDtypeStruct((3, N, 8, T), F32),
            jax.ShapeDtypeStruct((N, 4, T), F32),
        ),
        in_specs=[in_vmem, in_vmem, in_vmem],
        out_specs=(in_vmem, in_vmem),
        name="finish",
    )(off, quad, diag)
    diag = diag.reshape(2, HALF, 4, T).transpose(0, 2, 1, 3).reshape(2, 4, HALF * T)
    return off.transpose(0, 2, 1, 3).reshape(24, 2 * HALF * T), diag


def solution(mesh):
    return jax.shard_map(
        per_device,
        mesh=mesh,
        in_specs=(P("row", "col"), P(("row", "col"), None), P(None, ("row", "col"), None), P()),
        out_specs=(P(("row", "col"), None), P(None, ("row", "col"), None)),
        check_vma=False,
    )
```

```python
import jax
import jax.numpy as jnp
from jax import lax
from jax.experimental import pallas as pl
from jax.experimental.pallas import tpu as pltpu
from jax.sharding import PartitionSpec as P

MESH = pl.DeviceIdType.MESH
F32 = jnp.float32
BF16 = jnp.bfloat16
N = 16
HALF = 8
NT = 48
NA = 6
T = 128
CH = ((0, 1), (1, 3))

X4, Q5, S2, S3, P1, P2, X3, Y4, Q4, O4, O5, D5, S1 = range(13)


def split(x):
    high = x.astype(BF16)
    return high, (x - high.astype(F32)).astype(BF16)


def dot3(a, b):
    ah, al = a
    bh, bl = b
    dot = lambda u, v: jnp.dot(u, v, preferred_element_type=F32)
    return dot(ah, bh) + (dot(ah, bl) + dot(al, bh))


def kernel(
    anc_hbm,
    sep_hbm,
    pan_hbm,
    off,
    quad,
    place,
    s_rows,
    s_by_tile,
    s_col,
    s_tiles,
    s_unit,
    s_fin,
    p_cols,
    p_send,
    p_perm,
    p_unit,
    x_buf,
    x_t,
    y_unit,
    y_buf,
    q_unit,
    q_buf,
    off_st,
    off_cols,
    d_st,
    anc,
    sep,
    pan,
    fetch,
    send,
    recv,
):
    r = lax.axis_index("row")
    c = lax.axis_index("col")
    s = lax.div(r, HALF)
    b = lax.rem(r, HALF)
    chip = lax.div(c, 2)
    core = lax.rem(c, 2)
    sibling = c + 1 - 2 * core

    def remote(src, dst, i, device):
        return pltpu.make_async_remote_copy(
            src_ref=src,
            dst_ref=dst,
            send_sem=send.at[i],
            recv_sem=recv.at[i],
            device_id=device,
            device_id_type=MESH,
        )

    def local(src, dst, i):
        return pltpu.make_async_copy(src, dst, recv.at[i])

    def push(src, dst, i, dr, dc):
        here = jnp.logical_and(dr == r, dc == c)

        @pl.when(here)
        def _():
            local(src, dst, i).start()

        @pl.when(jnp.logical_not(here))
        def _():
            remote(src, dst, i, (dr, dc)).start()

    def take(sem, ref):
        pltpu.make_async_copy(ref, ref, sem).wait()

    def loop(lo, hi, body):
        def step(i, carry):
            body(i)
            return carry

        lax.fori_loop(lo, hi, step, 0)

    def over_col(i):
        j = N - 1 - i
        half, along, core = lax.div(j, 8), lax.rem(lax.div(j, 2), 4), lax.rem(j, 2)
        along = lax.div(along * (along + 1), 2)
        return (
            8 * lax.rem(lax.div(c, 8) + half, 2)
            + 2 * lax.rem(lax.div(c, 2) + along, 4)
            + lax.rem(c + core, 2)
        )

    def over_chips(i):
        j = HALF - 1 - i
        half, along = lax.div(j, 4), lax.rem(j, 4)
        along = lax.div(along * (along + 1), 2)
        return 8 * lax.rem(lax.div(c, 8) + half, 2) + 2 * lax.rem(chip + along, 4) + core

    def over_row(i):
        j = lax.div(i, 2)
        z = 4 + (1 - 2 * lax.rem(j, 2)) * lax.div(j + 1, 2)
        return 2 * lax.rem(lax.div(r, 2) + z, HALF) + lax.rem(r + 1 + i, 2)

    def over_half(i):
        j = 3 - lax.div(i, 2)
        z = lax.div(j * (j + 1), 2)
        return HALF * s + 2 * lax.rem(lax.div(b, 2) + z, 4) + lax.rem(b + 1 + i, 2)

    barrier = pltpu.get_barrier_semaphore()

    def greet(i):
        for device in ((r, over_col(i)), (over_row(i), c)):
            pl.semaphore_signal(barrier, inc=1, device_id=device, device_id_type=MESH)

    loop(0, N - 1, greet)
    for m in range(3):
        pltpu.make_async_copy(sep_hbm.at[m], sep.at[m], fetch.at[m]).start()
    pltpu.make_async_copy(pan_hbm, pan, fetch.at[3]).start()
    pltpu.make_async_copy(anc_hbm, anc, fetch.at[4]).start()
    for m in range(3):
        take(fetch.at[m], sep.at[m])
    take(fetch.at[3], pan)
    pltpu.make_async_copy(anc_hbm, anc, fetch.at[4]).wait()
    pl.semaphore_wait(barrier, 2 * (N - 1))

    for lo, hi in CH:

        def send_s(i, lo=lo, hi=hi):
            d = over_col(i)
            src = sep.at[pl.ds(lo, hi - lo), pl.ds(8 * d, 8), :]
            remote(src, s_rows.at[pl.ds(lo, hi - lo), c], S1 + lo, (r, d)).start()

        loop(0, N - 1, send_s)
        src = sep.at[pl.ds(lo, hi - lo), pl.ds(8 * c, 8), :]
        local(src, s_rows.at[pl.ds(lo, hi - lo), c], S1 + lo).start()

    def columns(d):
        return pan.at[:, :, pl.ds(pl.multiple_of(T * d, T), T)]

    def send_p(i):
        d = over_row(i)
        remote(columns(d), p_cols.at[r], P1, (d, c)).start()

    loop(0, N - 1, send_p)
    local(columns(r), p_cols.at[r], P1).start()

    row_of = []
    for k in range(NA):
        value = 0
        for j in range(1, N):
            value += (anc[s, k] >= 3 * j).astype(jnp.int32)
        row_of.append(value)
    for t in range(NT):
        value = NA
        for k in range(NA):
            value = jnp.minimum(value, NA - (anc[s, k] == t).astype(jnp.int32) * (NA - k))
        place[t] = value

    take(recv.at[P1], p_cols)
    for k in range(NA):
        for q in range(3):
            p_send[q, k] = p_cols[row_of[k], q]

    def send_p2(q):
        piece = 3 * c + q
        push(p_send.at[q], p_perm.at[lax.div(piece, N)], P2, r, lax.rem(piece, N))

    loop(0, 3, send_p2)

    for lo, hi in CH:
        take(recv.at[S1 + lo], s_rows.at[pl.ds(lo, hi - lo)])
        for m in range(lo, hi):
            for j in range(N):
                for v in range(3):
                    s_by_tile[m, 3 * j + v] = s_rows[m, j, :, T * v : T * v + T]
            for t in range(2):
                for l in range(NA):
                    s_col[t, l, m] = s_by_tile[m, anc[t, l]]

        def send_s2(i, lo=lo, hi=hi):
            d = over_row(i)
            l = lax.rem(d, HALF)

            @pl.when(l < NA)
            def _():
                src = s_col.at[lax.div(d, HALF), l, pl.ds(lo, hi - lo)]
                remote(src, s_tiles.at[pl.ds(3 * r + lo, hi - lo)], S2, (d, c)).start()

        loop(0, N - 1, send_s2)

        @pl.when(b < NA)
        def _():
            src = s_col.at[s, b, pl.ds(lo, hi - lo)]
            local(src, s_tiles.at[pl.ds(3 * r + lo, hi - lo)], S2).start()

    take(recv.at[P2], p_perm)
    for k in range(NA):
        p_unit[k] = p_perm[anc[s, k] - 3 * row_of[k], k]

    def send_x(i):
        d = over_chips(i)
        remote(p_unit, x_buf.at[:, chip, core], X3, (r, d)).start()

    loop(0, HALF - 1, send_x)
    x_buf[:, pl.ds(chip, 1), pl.ds(core, 1)] = p_unit[...][:, None, None]

    @pl.when(b < NA)
    def _():
        take(recv.at[S2], s_tiles)
        for k in range(NA):
            s_unit[k] = s_tiles[anc[s, k]]

        def send_s3(i):
            d = over_half(i)
            remote(s_unit, s_fin.at[b], S3, (d, c)).start()

        loop(0, HALF - 1, send_s3)
        local(s_unit, s_fin.at[b], S3).start()

    take(recv.at[X3], x_buf.at[:, pl.ds(0, HALF - 1), 0])
    remote(x_buf.at[:, :, core], x_buf.at[:, :, core], X4, (r, sibling)).start()
    take(recv.at[X4], x_buf.at[:, :, 0])
    for k in range(NA):
        x_t[:, :, T * k : T * (k + 1)] = x_buf[k].reshape(T, T).T.reshape(2 * N, 4, T)
    y_unit[0:4] = x_t[c]
    y_unit[4:8] = x_t[N + c]

    def send_y4(i):
        d = over_half(i)
        remote(y_unit, y_buf.at[b], Y4, (d, c)).start()

    loop(0, HALF - 1, send_y4)
    local(y_unit, y_buf.at[b], Y4).start()

    take(recv.at[S3], s_fin)
    acc = jnp.zeros((NA * 8, T), F32)
    for l in range(NA):
        acc += dot3(split(s_fin[l].reshape(NA * 8, T)), split(x_buf[l].reshape(T, T)))
    q_unit[0:NA] = acc.reshape(NA, 8, T)
    q_unit[NA] = jnp.zeros((8, T), F32)

    def send_q(i):
        d = over_chips(i)
        remote(q_unit.at[pl.ds(0, NA)], q_buf.at[:, chip, core], Q4, (r, d)).start()

    loop(0, HALF - 1, send_q)
    q_buf[:, pl.ds(chip, 1), pl.ds(core, 1)] = q_unit[0:NA][:, None, None]

    for t in range(NT):
        off_st[t] = -q_unit[place[t]]

    def send_off(i):
        d = over_row(i)
        remote(off_st.at[pl.ds(3 * d, 3)], off_cols.at[r], O4, (d, c)).start()

    loop(0, N - 1, send_off)
    local(off_st.at[pl.ds(3 * r, 3)], off_cols.at[r], O4).start()

    take(recv.at[Y4], y_buf)
    y_halves = split(y_buf[...].reshape(HALF * 8, NA * T))
    take(recv.at[Q4], q_buf.at[:, pl.ds(0, HALF - 1), 0])
    remote(q_buf.at[:, :, core], q_buf.at[:, :, core], Q5, (r, sibling)).start()
    take(recv.at[Q5], q_buf.at[:, :, 0])

    acc = dot3(y_halves, split(q_buf[...].reshape(NA * T, T)))
    d_st[...] = acc.reshape(N, 4, T)

    def send_d(i):
        d = over_row(i)
        remote(d_st.at[d], quad.at[r], D5, (d, c)).start()

    loop(0, N - 1, send_d)
    local(d_st.at[r], quad.at[r], D5).start()

    take(recv.at[O4], off_cols)

    def send_off2(m):
        piece = N * m + c
        push(off_cols.at[:, m], off.at[lax.rem(piece, 3)], O5, r, lax.div(piece, 3))

    loop(0, 3, send_off2)

    for lo, hi in CH:
        take(send.at[S1 + lo], s_rows.at[pl.ds(lo, hi - lo), pl.ds(0, N - 1)])
    take(send.at[P1], p_cols.at[pl.ds(0, N - 1)])
    take(send.at[X3], x_buf.at[:, pl.ds(0, HALF - 1), 0])
    take(send.at[X4], x_buf.at[:, :, 0])
    take(send.at[Y4], y_buf.at[pl.ds(0, HALF - 1)])
    take(send.at[Q4], q_buf.at[:, pl.ds(0, HALF - 1), 0])
    take(send.at[Q5], q_buf.at[:, :, 0])
    take(send.at[O4], off_cols.at[pl.ds(0, N - 1)])
    take(send.at[D5], d_st.at[pl.ds(0, N - 1)])

    @pl.when(b < NA)
    def _():
        take(send.at[S3], s_tiles.at[pl.ds(0, 7 * NA)])
        take(send.at[S2], s_tiles.at[pl.ds(0, 33)])

    @pl.when(b >= NA)
    def _():
        take(send.at[S2], s_tiles.at[pl.ds(0, 36)])

    own = jnp.logical_or(jnp.logical_or(c == 0, c == 7), jnp.logical_or(c == 8, c == 15))

    @pl.when(own)
    def _():
        take(send.at[P2], p_perm.at[pl.ds(0, 2)])
        take(send.at[O5], off_st.at[pl.ds(0, 2 * N)])

    @pl.when(jnp.logical_not(own))
    def _():
        take(send.at[P2], p_perm)
        take(send.at[O5], off_st)

    take(recv.at[O5], off)
    take(recv.at[D5], quad)


def finish(off, quad, diag, off_out, diag_out):
    off_out[...] = off[...]
    diag_out[...] = diag[...] + quad[...]


def per_device(separator_inverse, panels, diag_inverse, ancestors):
    hbm = pl.BlockSpec(memory_space=pl.ANY)
    vmem = pltpu.VMEM
    off, quad = pl.pallas_call(
        kernel,
        out_shape=(
            jax.ShapeDtypeStruct((3, N, 8, T), F32),
            jax.ShapeDtypeStruct((N, 4, T), F32),
        ),
        in_specs=[hbm, hbm, hbm],
        out_specs=(hbm, hbm),
        scratch_shapes=[
            pltpu.SMEM((NT,), jnp.int32),
            vmem((3, N, 8, 3 * T), F32),
            vmem((3, NT, 8, T), F32),
            vmem((2, NA, 3, 8, T), F32),
            vmem((NT, 8, T), F32),
            vmem((NA, 8, T), F32),
            vmem((NA, NA, 8, T), F32),
            vmem((N, 3, 8, T), F32),
            vmem((3, NA, 8, T), F32),
            vmem((3, NA, 8, T), F32),
            vmem((NA, 8, T), F32),
            vmem((NA, HALF, 2, 8, T), F32),
            vmem((2 * N, 4, NA * T), F32),
            vmem((8, NA * T), F32),
            vmem((HALF, 8, NA * T), F32),
            vmem((NA + 1, 8, T), F32),
            vmem((NA, HALF, 2, 8, T), F32),
            vmem((NT, 8, T), F32),
            vmem((N, 3, 8, T), F32),
            vmem((N, 4, T), F32),
            pltpu.SMEM((2, NA), jnp.int32),
            vmem((3, T, 3 * T), F32),
            vmem((3, 8, 2 * HALF * T), F32),
            pltpu.SemaphoreType.DMA((5,)),
            pltpu.SemaphoreType.DMA((15,)),
            pltpu.SemaphoreType.DMA((15,)),
        ],
        compiler_params=pltpu.CompilerParams(collective_id=0, has_side_effects=True),
        name="selected_inverse",
    )(
        ancestors,
        separator_inverse.reshape(3, T, 3 * T),
        panels.reshape(3, 8, 2 * HALF * T),
    )
    diag = diag_inverse.reshape(2, 4, HALF, T).transpose(0, 2, 1, 3).reshape(N, 4, T)
    in_vmem = pl.BlockSpec(memory_space=pltpu.VMEM)
    off, diag = pl.pallas_call(
        finish,
        out_shape=(
            jax.ShapeDtypeStruct((3, N, 8, T), F32),
            jax.ShapeDtypeStruct((N, 4, T), F32),
        ),
        in_specs=[in_vmem, in_vmem, in_vmem],
        out_specs=(in_vmem, in_vmem),
        name="finish",
    )(off, quad, diag)
    diag = diag.reshape(2, HALF, 4, T).transpose(0, 2, 1, 3).reshape(2, 4, HALF * T)
    return off.transpose(0, 2, 1, 3).reshape(24, 2 * HALF * T), diag


def solution(mesh):
    return jax.shard_map(
        per_device,
        mesh=mesh,
        in_specs=(P("row", "col"), P(("row", "col"), None), P(None, ("row", "col"), None), P()),
        out_specs=(P(("row", "col"), None), P(None, ("row", "col"), None)),
        check_vma=False,
    )
```

```python
import jax
import jax.numpy as jnp
from jax import lax
from jax.experimental import pallas as pl
from jax.experimental.pallas import tpu as pltpu
from jax.sharding import PartitionSpec as P

MESH = pl.DeviceIdType.MESH
F32 = jnp.float32
BF16 = jnp.bfloat16
N = 16
HALF = 8
NT = 48
NA = 6
T = 128
CH = ((0, 1), (1, 3))

X4, Q5, S2, S3, P1, P2, X3, Y4, Q4, O4, O5, D5, S1 = range(13)


def split(x):
    high = x.astype(BF16)
    return high, (x - high.astype(F32)).astype(BF16)


def dot3(a, b):
    ah, al = a
    bh, bl = b
    dot = lambda u, v: jnp.dot(u, v, preferred_element_type=F32)
    return dot(ah, bh) + (dot(ah, bl) + dot(al, bh))


def kernel(
    anc_hbm,
    sep_hbm,
    pan_hbm,
    off,
    quad,
    place,
    s_rows,
    s_by_tile,
    s_col,
    s_tiles,
    s_unit,
    s_fin,
    p_cols,
    p_send,
    p_perm,
    p_unit,
    x_buf,
    x_t,
    y_unit,
    y_buf,
    q_unit,
    q_buf,
    off_st,
    off_cols,
    d_st,
    anc,
    sep,
    pan,
    fetch,
    send,
    recv,
):
    r = lax.axis_index("row")
    c = lax.axis_index("col")
    s = lax.div(r, HALF)
    b = lax.rem(r, HALF)
    chip = lax.div(c, 2)
    core = lax.rem(c, 2)
    sibling = c + 1 - 2 * core

    def remote(src, dst, i, device):
        return pltpu.make_async_remote_copy(
            src_ref=src,
            dst_ref=dst,
            send_sem=send.at[i],
            recv_sem=recv.at[i],
            device_id=device,
            device_id_type=MESH,
        )

    def local(src, dst, i):
        return pltpu.make_async_copy(src, dst, recv.at[i])

    def push(src, dst, i, dr, dc):
        here = jnp.logical_and(dr == r, dc == c)

        @pl.when(here)
        def _():
            local(src, dst, i).start()

        @pl.when(jnp.logical_not(here))
        def _():
            remote(src, dst, i, (dr, dc)).start()

    def take(sem, ref):
        pltpu.make_async_copy(ref, ref, sem).wait()

    def loop(lo, hi, body):
        def step(i, carry):
            body(i)
            return carry

        lax.fori_loop(lo, hi, step, 0)

    def over_col(i):
        j = N - 1 - i
        half, along, core = lax.div(j, 8), lax.rem(lax.div(j, 2), 4), lax.rem(j, 2)
        along = lax.div(along * (along + 1), 2)
        return (
            8 * lax.rem(lax.div(c, 8) + half, 2)
            + 2 * lax.rem(lax.div(c, 2) + along, 4)
            + lax.rem(c + core, 2)
        )

    def over_chips(i):
        j = HALF - 1 - i
        half, along = lax.div(j, 4), lax.rem(j, 4)
        along = lax.div(along * (along + 1), 2)
        return 8 * lax.rem(lax.div(c, 8) + half, 2) + 2 * lax.rem(chip + along, 4) + core

    def over_row(i):
        j = lax.div(i, 2)
        z = 4 + (1 - 2 * lax.rem(j, 2)) * lax.div(j + 1, 2)
        return 2 * lax.rem(lax.div(r, 2) + z, HALF) + lax.rem(r + 1 + i, 2)

    def over_half(i):
        j = 3 - lax.div(i, 2)
        z = lax.div(j * (j + 1), 2)
        return HALF * s + 2 * lax.rem(lax.div(b, 2) + z, 4) + lax.rem(b + 1 + i, 2)

    def tile(buf, k):
        return jnp.concatenate([buf[o % 2, o // 2, k] for o in range(N)])

    barrier = pltpu.get_barrier_semaphore()

    def greet(i):
        for device in ((r, over_col(i)), (over_row(i), c)):
            pl.semaphore_signal(barrier, inc=1, device_id=device, device_id_type=MESH)

    loop(0, N - 1, greet)
    for m in range(3):
        pltpu.make_async_copy(sep_hbm.at[m], sep.at[m], fetch.at[m]).start()
    pltpu.make_async_copy(pan_hbm, pan, fetch.at[3]).start()
    pltpu.make_async_copy(anc_hbm, anc, fetch.at[4]).start()
    for m in range(3):
        take(fetch.at[m], sep.at[m])
    take(fetch.at[3], pan)
    pltpu.make_async_copy(anc_hbm, anc, fetch.at[4]).wait()
    pl.semaphore_wait(barrier, 2 * (N - 1))

    for lo, hi in CH:

        def send_s(i, lo=lo, hi=hi):
            d = over_col(i)
            src = sep.at[pl.ds(lo, hi - lo), pl.ds(8 * d, 8), :]
            remote(src, s_rows.at[pl.ds(lo, hi - lo), c], S1 + lo, (r, d)).start()

        loop(0, N - 1, send_s)
        src = sep.at[pl.ds(lo, hi - lo), pl.ds(8 * c, 8), :]
        local(src, s_rows.at[pl.ds(lo, hi - lo), c], S1 + lo).start()

    def columns(d):
        return pan.at[:, :, pl.ds(pl.multiple_of(T * d, T), T)]

    def send_p(i):
        d = over_row(i)
        remote(columns(d), p_cols.at[r], P1, (d, c)).start()

    loop(0, N - 1, send_p)
    local(columns(r), p_cols.at[r], P1).start()

    row_of = []
    for k in range(NA):
        value = 0
        for j in range(1, N):
            value += (anc[s, k] >= 3 * j).astype(jnp.int32)
        row_of.append(value)
    for t in range(NT):
        value = NA
        for k in range(NA):
            value = jnp.minimum(value, NA - (anc[s, k] == t).astype(jnp.int32) * (NA - k))
        place[t] = value

    take(recv.at[P1], p_cols)
    for k in range(NA):
        for q in range(3):
            p_send[q, k] = p_cols[row_of[k], q]

    def send_p2(q):
        piece = 3 * c + q
        push(p_send.at[q], p_perm.at[lax.div(piece, N)], P2, r, lax.rem(piece, N))

    loop(0, 3, send_p2)

    for lo, hi in CH:
        take(recv.at[S1 + lo], s_rows.at[pl.ds(lo, hi - lo)])
        for m in range(lo, hi):
            for j in range(N):
                for v in range(3):
                    s_by_tile[m, 3 * j + v] = s_rows[m, j, :, T * v : T * v + T]
            for t in range(2):
                for l in range(NA):
                    s_col[t, l, m] = s_by_tile[m, anc[t, l]]

        def send_s2(i, lo=lo, hi=hi):
            d = over_row(i)
            l = lax.rem(d, HALF)

            @pl.when(l < NA)
            def _():
                src = s_col.at[lax.div(d, HALF), l, pl.ds(lo, hi - lo)]
                remote(src, s_tiles.at[pl.ds(3 * r + lo, hi - lo)], S2, (d, c)).start()

        loop(0, N - 1, send_s2)

        @pl.when(b < NA)
        def _():
            src = s_col.at[s, b, pl.ds(lo, hi - lo)]
            local(src, s_tiles.at[pl.ds(3 * r + lo, hi - lo)], S2).start()

    take(recv.at[P2], p_perm)
    for k in range(NA):
        p_unit[k] = p_perm[anc[s, k] - 3 * row_of[k], k]

    def send_x(i):
        d = over_chips(i)
        remote(p_unit, x_buf.at[core, chip], X3, (r, d)).start()

    loop(0, HALF - 1, send_x)
    x_buf[core, chip] = p_unit[...]

    @pl.when(b < NA)
    def _():
        take(recv.at[S2], s_tiles)
        for k in range(NA):
            s_unit[k] = s_tiles[anc[s, k]]

        def send_s3(i):
            d = over_half(i)
            remote(s_unit, s_fin.at[b], S3, (d, c)).start()

        loop(0, HALF - 1, send_s3)
        local(s_unit, s_fin.at[b], S3).start()

    take(recv.at[X3], x_buf.at[0, pl.ds(0, HALF - 1)])
    remote(x_buf.at[core], x_buf.at[core], X4, (r, sibling)).start()
    take(recv.at[X4], x_buf.at[0])
    for k in range(NA):
        x_t[:, :, T * k : T * (k + 1)] = tile(x_buf, k).T.reshape(2 * N, 4, T)
    y_unit[0:4] = x_t[c]
    y_unit[4:8] = x_t[N + c]

    def send_y4(i):
        d = over_half(i)
        remote(y_unit, y_buf.at[b], Y4, (d, c)).start()

    loop(0, HALF - 1, send_y4)
    local(y_unit, y_buf.at[b], Y4).start()

    take(recv.at[S3], s_fin)
    acc = jnp.zeros((NA * 8, T), F32)
    for l in range(NA):
        acc += dot3(split(s_fin[l].reshape(NA * 8, T)), split(tile(x_buf, l)))
    q_unit[0:NA] = acc.reshape(NA, 8, T)
    q_unit[NA] = jnp.zeros((8, T), F32)

    def send_q(i):
        d = over_chips(i)
        remote(q_unit.at[pl.ds(0, NA)], q_buf.at[core, chip], Q4, (r, d)).start()

    loop(0, HALF - 1, send_q)
    q_buf[core, chip] = q_unit[0:NA]

    for t in range(NT):
        off_st[t] = -q_unit[place[t]]

    def send_off(i):
        d = over_row(i)
        remote(off_st.at[pl.ds(3 * d, 3)], off_cols.at[r], O4, (d, c)).start()

    loop(0, N - 1, send_off)
    local(off_st.at[pl.ds(3 * r, 3)], off_cols.at[r], O4).start()

    take(recv.at[Q4], q_buf.at[0, pl.ds(0, HALF - 1)])
    remote(q_buf.at[core], q_buf.at[core], Q5, (r, sibling)).start()
    take(recv.at[Y4], y_buf)
    y_halves = split(y_buf[...].reshape(HALF * 8, NA * T))
    take(recv.at[Q5], q_buf.at[0])

    acc = dot3(y_halves, split(jnp.concatenate([tile(q_buf, k) for k in range(NA)])))
    d_st[...] = acc.reshape(N, 4, T)

    def send_d(i):
        d = over_row(i)
        remote(d_st.at[d], quad.at[r], D5, (d, c)).start()

    loop(0, N - 1, send_d)
    local(d_st.at[r], quad.at[r], D5).start()

    take(recv.at[O4], off_cols)

    def send_off2(m):
        piece = N * m + c
        push(off_cols.at[:, m], off.at[lax.rem(piece, 3)], O5, r, lax.div(piece, 3))

    loop(0, 3, send_off2)

    for lo, hi in CH:
        take(send.at[S1 + lo], s_rows.at[pl.ds(lo, hi - lo), pl.ds(0, N - 1)])
    take(send.at[P1], p_cols.at[pl.ds(0, N - 1)])
    take(send.at[X3], x_buf.at[0, pl.ds(0, HALF - 1)])
    take(send.at[X4], x_buf.at[0])
    take(send.at[Y4], y_buf.at[pl.ds(0, HALF - 1)])
    take(send.at[Q4], q_buf.at[0, pl.ds(0, HALF - 1)])
    take(send.at[Q5], q_buf.at[0])
    take(send.at[O4], off_cols.at[pl.ds(0, N - 1)])
    take(send.at[D5], d_st.at[pl.ds(0, N - 1)])

    @pl.when(b < NA)
    def _():
        take(send.at[S3], s_tiles.at[pl.ds(0, 7 * NA)])
        take(send.at[S2], s_tiles.at[pl.ds(0, 33)])

    @pl.when(b >= NA)
    def _():
        take(send.at[S2], s_tiles.at[pl.ds(0, 36)])

    own = jnp.logical_or(jnp.logical_or(c == 0, c == 7), jnp.logical_or(c == 8, c == 15))

    @pl.when(own)
    def _():
        take(send.at[P2], p_perm.at[pl.ds(0, 2)])
        take(send.at[O5], off_st.at[pl.ds(0, 2 * N)])

    @pl.when(jnp.logical_not(own))
    def _():
        take(send.at[P2], p_perm)
        take(send.at[O5], off_st)

    take(recv.at[O5], off)
    take(recv.at[D5], quad)


def finish(off, quad, diag, off_out, diag_out):
    off_out[...] = off[...]
    diag_out[...] = diag[...] + quad[...]


def per_device(separator_inverse, panels, diag_inverse, ancestors):
    hbm = pl.BlockSpec(memory_space=pl.ANY)
    vmem = pltpu.VMEM
    off, quad = pl.pallas_call(
        kernel,
        out_shape=(
            jax.ShapeDtypeStruct((3, N, 8, T), F32),
            jax.ShapeDtypeStruct((N, 4, T), F32),
        ),
        in_specs=[hbm, hbm, hbm],
        out_specs=(hbm, hbm),
        scratch_shapes=[
            pltpu.SMEM((NT,), jnp.int32),
            vmem((3, N, 8, 3 * T), F32),
            vmem((3, NT, 8, T), F32),
            vmem((2, NA, 3, 8, T), F32),
            vmem((NT, 8, T), F32),
            vmem((NA, 8, T), F32),
            vmem((NA, NA, 8, T), F32),
            vmem((N, 3, 8, T), F32),
            vmem((3, NA, 8, T), F32),
            vmem((3, NA, 8, T), F32),
            vmem((NA, 8, T), F32),
            vmem((2, HALF, NA, 8, T), F32),
            vmem((2 * N, 4, NA * T), F32),
            vmem((8, NA * T), F32),
            vmem((HALF, 8, NA * T), F32),
            vmem((NA + 1, 8, T), F32),
            vmem((2, HALF, NA, 8, T), F32),
            vmem((NT, 8, T), F32),
            vmem((N, 3, 8, T), F32),
            vmem((N, 4, T), F32),
            pltpu.SMEM((2, NA), jnp.int32),
            vmem((3, T, 3 * T), F32),
            vmem((3, 8, 2 * HALF * T), F32),
            pltpu.SemaphoreType.DMA((5,)),
            pltpu.SemaphoreType.DMA((15,)),
            pltpu.SemaphoreType.DMA((15,)),
        ],
        compiler_params=pltpu.CompilerParams(collective_id=0, has_side_effects=True),
        name="selected_inverse",
    )(
        ancestors,
        separator_inverse.reshape(3, T, 3 * T),
        panels.reshape(3, 8, 2 * HALF * T),
    )
    diag = diag_inverse.reshape(2, 4, HALF, T).transpose(0, 2, 1, 3).reshape(N, 4, T)
    in_vmem = pl.BlockSpec(memory_space=pltpu.VMEM)
    off, diag = pl.pallas_call(
        finish,
        out_shape=(
            jax.ShapeDtypeStruct((3, N, 8, T), F32),
            jax.ShapeDtypeStruct((N, 4, T), F32),
        ),
        in_specs=[in_vmem, in_vmem, in_vmem],
        out_specs=(in_vmem, in_vmem),
        name="finish",
    )(off, quad, diag)
    diag = diag.reshape(2, HALF, 4, T).transpose(0, 2, 1, 3).reshape(2, 4, HALF * T)
    return off.transpose(0, 2, 1, 3).reshape(24, 2 * HALF * T), diag


def solution(mesh):
    return jax.shard_map(
        per_device,
        mesh=mesh,
        in_specs=(P("row", "col"), P(("row", "col"), None), P(None, ("row", "col"), None), P()),
        out_specs=(P(("row", "col"), None), P(None, ("row", "col"), None)),
        check_vma=False,
    )
```
